32 devices in a mesh: mem: 4 (over x, core), tile: 8 (over z, y).
Axes of the slice: x: 2, y: 2, z: 4, core: 2. Of those that a mesh axis runs over, the one named last changes fastest.
Arguments:
- background: bfloat16 [512, 4, 8, 1024], P('mem', None, 'tile'), may hold values from -6 to 6
- evolved: bfloat16 [512, 32768], P('mem', 'tile'), may hold values from -6 to 6
- obs_value: bfloat16 [32768], P('tile'), may hold values from -8 to 8
- obs_var: bfloat16 [32768], P('tile'), may hold values from 0.5 to 2
- obs_patch: int32 [32768, 1], P('tile'), may hold values from 0 to 31; in each aligned block of 4096 rows (0 to 4095, 4096 to 8191, ...) at most 256 rows name the same one
- obs_pos: int32 [32768], P('tile'), may hold values from 0 to 127
Outputs:
- analysis: bfloat16 [512, 4, 8, 1024], P('mem', None, 'tile')
The draws below stay inside these ranges and needn't reach their ends.
Inputs may be any that keep to these rules, and one draw needn't show every extreme that they name: `obs_patch`: in each aligned block of 4096 rows (the observations of one tile index) no patch is named by more than 256 rows, a bound that some block reaches.
All inputs are finite; a program needn't handle non-finite values.
Results may differ from the reference program's by a relative error of at most 0.0065.
Values may be sent and summed in bfloat16 or wider, within the bound.
A program may use at most 64 MiB of HBM per device.

```python
import math
import jax
import jax.numpy as jnp
import numpy as np
from jax import lax

MEMBERS = 512
PATCH_CELLS = 128
ITERS = 4
PATCHES = 32
CELLS = 1024
SLOTS = 2048
CAPACITY = 256
OBS_DEV = 4096
OBS_ALL = 32768
N_MEM = 4
N_TILE = 8


def plant(values, key, least, high):
    longest = values.shape.index(max(values.shape))
    spots = []
    for shift in (0, 1):
        where = [jax.random.randint(jax.random.fold_in(key, axis), (), 0, length) for axis, length in enumerate(values.shape)]
        where[longest] = (where[longest] + shift) % values.shape[longest]
        spots.append(tuple(where))
    return values.at[spots[0]].set(least).at[spots[1]].set(high)


def levels(key, dims, split, low, largest):
    def one(axis_at, parts):
        heights = jax.random.uniform(jax.random.fold_in(jax.random.fold_in(key, 6), axis_at), (parts,), jnp.float32, low / len(split), largest / len(split))
        return jnp.repeat(jnp.exp(heights), dims[axis_at] // parts).reshape((-1,) + (1,) * (len(dims) - axis_at - 1))

    level = one(*split[0])
    for cut in split[1:]:
        level = level * one(*cut)
    return level


def routed_block(stream_key, own, number, rows, amount, top, reach, slope):
    order = jax.random.permutation(stream_key, amount)
    packed, usual = load_shares(amount, rows * top, reach, slope, True), load_shares(amount, rows * top, reach, slope, False)
    places = jnp.arange(amount)

    def named(tallies, turn):
        used = int((tallies > 0).sum())
        fixed = max(1, used // 4)
        moved = fixed + (places - fixed + turn * (used - fixed)) % max(1, amount - fixed)
        return jnp.zeros((amount,), jnp.int32).at[order[jnp.where(places < fixed, places, moved)]].set(jnp.asarray(tallies, jnp.int32))

    tallies = jnp.where(number % 4 == 0, named(packed, number // 4), named(usual, number - number // 4 - 1))
    mixed = jax.random.permutation(jax.random.fold_in(own, 3), amount)
    giver, taker = mixed[0:amount // 2 * 2:2], mixed[1:amount // 2 * 2:2]
    slack = jnp.minimum(tallies[giver] - 1, reach - tallies[taker]) // 2
    slack = jnp.where((giver == order[0]) | (taker == order[0]) | (tallies[taker] == 0), 0, jnp.maximum(slack, 0))
    moved = jax.random.randint(jax.random.fold_in(own, 4), (amount // 2,), 0, 1 << 20) % (slack + 1)
    tallies = tallies.at[giver].add(-moved).at[taker].add(moved)
    items = jnp.searchsorted(jnp.cumsum(tallies), jnp.arange(rows * top), side="right").astype(jnp.int32)
    listing = items.reshape(top, rows).T
    listing = listing[jax.random.permutation(jax.random.fold_in(own, 1), rows)]
    turn = jax.random.randint(jax.random.fold_in(own, 2), (rows, 1), 0, top)
    return jnp.take_along_axis(listing, (jnp.arange(top)[None, :] + turn) % top, axis=1)


def load_shares(number_of, total, limit, slope, full):
    portions = [(1 << 20) // math.isqrt(standing ** slope) + 1 for standing in range(1, number_of + 1)]
    largest = limit if full else min(limit, max(-(-total // number_of), total * portions[0] // sum(portions)))
    least = 1 if total - largest >= number_of - 1 else 0
    given, spare = [largest] + [least] * (number_of - 1), total - largest - least * (number_of - 1)
    while spare > 0:
        candidates = [i for i in range(1, number_of) if given[i] < largest] or [i for i in range(1, number_of) if given[i] < limit]
        mass, budget = sum([portions[i] for i in candidates]), spare
        for i in candidates:
            more = min(limit - given[i], max(1, budget * portions[i] // mass), spare)
            given[i] = given[i] + more
            spare = spare - more
    return np.array(given)


def normal_values(stream_key, shape, scale, most, cuts=(), kind=jnp.bfloat16):
    factor_of = levels(stream_key, shape, cuts, -0.22, 0.18) if cuts else 1.0
    values = jax.random.normal(stream_key, shape, jnp.float32) * scale * factor_of
    return jnp.minimum(jnp.maximum(values, -most), most).astype(kind)


def setup_inputs(seed: int = 0) -> dict:
    key_list = jax.random.split(jax.random.key(seed), 7)
    background = normal_values(key_list[0], (MEMBERS, N_MEM, N_TILE, CELLS), 1.0, 6.0, ((0, 4), (2, 8)))
    evolved = normal_values(key_list[1], (MEMBERS, OBS_ALL), 1.0, 6.0, ((0, 4), (1, 8)))
    obs_value = normal_values(key_list[2], (OBS_ALL,), 1.5, 8.0, ((0, 8),))
    obs_var = jnp.clip(jnp.exp(math.log(2.0) - 1.3862944 * jax.random.uniform(key_list[3], (OBS_ALL,), jnp.float32) ** levels(key_list[3], (OBS_ALL,), ((0, 8),), -0.2, 0.2)), 0.5, 2.0).astype(jnp.bfloat16)
    obs_patch_keys = jax.random.split(jax.random.fold_in(key_list[4], 1), OBS_ALL // OBS_DEV)
    obs_patch_turns = jax.random.permutation(jax.random.fold_in(key_list[4], 3), OBS_ALL // OBS_DEV)
    obs_patch = jax.vmap(lambda own, number: routed_block(jax.random.fold_in(key_list[4], 2), own, number, OBS_DEV, PATCHES, 1, CAPACITY, 2))(obs_patch_keys, obs_patch_turns).reshape((OBS_ALL, 1))
    obs_pos = plant(jax.random.randint(key_list[5], (OBS_ALL,), 0, PATCH_CELLS), jax.random.fold_in(key_list[5], 1), 0, PATCH_CELLS - 1).astype(jnp.int32)
    return dict(background=background, evolved=evolved, obs_value=obs_value, obs_var=obs_var, obs_patch=obs_patch, obs_pos=obs_pos)


def localize(position, offset):
    distance = (offset * PATCH_CELLS + position + 0.5 - 0.5 * PATCH_CELLS) / PATCH_CELLS
    return jnp.exp(-2.0 * distance * distance)

def gram_terms(centred, innovation, weight, loc_weight):
    weighted = (centred.astype(jnp.float32) * (weight * loc_weight)[None, :]).astype(jnp.bfloat16)
    gram_mat = lax.dot_general(weighted, centred, (((1,), (1,)), ((), ())), preferred_element_type=jnp.float32)
    gram_vec = jnp.dot(weighted, innovation, preferred_element_type=jnp.float32)
    return (gram_mat, gram_vec)

def inverse_root(gram_mat):
    mat_size = gram_mat.shape[0]
    identity = jnp.eye(mat_size, dtype=jnp.float32)
    norm_scale = jnp.sqrt(jnp.sum(gram_mat * gram_mat))
    root_up = gram_mat / norm_scale
    root_down = identity
    for sweep_index in range(ITERS):
        middle = 1.5 * identity - 0.5 * jnp.dot(root_down, root_up, precision=lax.Precision.HIGHEST)
        root_up = jnp.dot(root_up, middle, precision=lax.Precision.HIGHEST)
        root_down = jnp.dot(middle, root_down, precision=lax.Precision.HIGHEST)
    return root_down / jnp.sqrt(norm_scale)

def transform(gram_mat, gram_vec):
    mat_size = gram_mat.shape[0]
    identity = jnp.eye(mat_size, dtype=jnp.float32)
    inv_root = inverse_root(gram_mat + (mat_size - 1.0) * identity)
    inner_w = jnp.dot(inv_root, gram_vec, precision=lax.Precision.HIGHEST)
    mean_w = jnp.dot(inv_root, inner_w, precision=lax.Precision.HIGHEST)
    return (math.sqrt(mat_size - 1.0) * inv_root + mean_w[:, None]).astype(jnp.bfloat16)

def update(states, transform_mat):
    members = states.shape[0]
    state_mean = lax.optimization_barrier(jnp.sum(states.astype(jnp.float32), 0)) / members
    deviation = (states.astype(jnp.float32) - state_mean[None, :]).astype(jnp.bfloat16)
    mixed = lax.dot_general(transform_mat, deviation, (((0,), (0,)), ((), ())), preferred_element_type=jnp.float32)
    return (state_mean[None, :] + mixed).astype(jnp.bfloat16)

def reference(background, evolved, obs_value, obs_var, obs_patch, obs_pos):
    obs_total = evolved.shape[1]
    target = obs_patch[:, 0]
    obs_mean = lax.optimization_barrier(jnp.sum(evolved.astype(jnp.float32), 0)) / MEMBERS
    centred = (evolved.astype(jnp.float32) - obs_mean[None, :]).astype(jnp.bfloat16)
    innovation = (obs_value.astype(jnp.float32) - obs_mean).astype(jnp.bfloat16)
    weight = 1.0 / obs_var.astype(jnp.float32)
    onehot = (target[:, None] == jnp.arange(PATCHES, dtype=jnp.int32)[None, :]).astype(jnp.int32)
    slot_rank = lax.optimization_barrier(jnp.sum(jnp.cumsum(onehot, 0) * onehot, 1)) - 1
    slot_place = (target * SLOTS + slot_rank).astype(jnp.int32)
    table = jnp.full((PATCHES * SLOTS,), obs_total, jnp.int32)
    table = table.at[slot_place].set(jnp.arange(obs_total, dtype=jnp.int32)).reshape(PATCHES, SLOTS)
    centred_pad = jnp.concatenate([centred, jnp.zeros((MEMBERS, 1), jnp.bfloat16)], 1)
    innovation_pad = jnp.concatenate([innovation, jnp.zeros((1,), jnp.bfloat16)])
    weight_pad = jnp.concatenate([weight, jnp.zeros((1,), jnp.float32)])
    position_pad = jnp.concatenate([obs_pos.astype(jnp.float32), jnp.zeros((1,), jnp.float32)])
    offset = jnp.repeat(jnp.array([-1.0, 0.0, 1.0], jnp.float32), SLOTS)

    def one_patch(patch_index):
        below = (patch_index + PATCHES - 1) % PATCHES
        above = (patch_index + 1) % PATCHES
        slot_rows = jnp.concatenate([table[below], table[patch_index], table[above]])
        gram_mat, gram_vec = gram_terms(centred_pad[:, slot_rows], innovation_pad[slot_rows], weight_pad[slot_rows], localize(position_pad[slot_rows], offset))
        transform_mat = transform(gram_mat, gram_vec)
        states = background[:, patch_index // N_TILE, patch_index % N_TILE, :]
        return update(states, transform_mat)
    result = lax.map(one_patch, jnp.arange(PATCHES, dtype=jnp.int32))
    return result.reshape(N_MEM, N_TILE, MEMBERS, CELLS).transpose(2, 0, 1, 3)
```

```python
import functools
import math

import jax
import jax.numpy as jnp
from jax import lax
from jax.experimental import pallas as pl
from jax.experimental.pallas import tpu as pltpu
from jax.sharding import PartitionSpec as P

PATCH_CELLS = 128
OBS_PATCH = 1024
INFO = 16
VMEM_LIMIT = 48 * 1024 * 1024
NT = (((1,), (1,)), ((), ()))


def dispatch_kernel(patches, capacity, data_ref, target_ref, out_ref, rank_ref):
    obs = data_ref.shape[1]
    chunk = 256
    upper = (
        lax.broadcasted_iota(jnp.int32, (chunk, chunk), 0)
        <= lax.broadcasted_iota(jnp.int32, (chunk, chunk), 1)
    ).astype(jnp.float32).astype(jnp.bfloat16)
    names = lax.broadcasted_iota(jnp.int32, (patches, chunk), 0)
    carry = jnp.zeros((patches, 1), jnp.float32)
    for start in range(0, obs, chunk):
        hit = names == target_ref[:, start : start + chunk]
        one = jnp.where(hit, 1.0, 0.0)
        run = jnp.dot(one.astype(jnp.bfloat16), upper, preferred_element_type=jnp.float32)
        rank_ref[:, start : start + chunk] = jnp.sum(one * (run + carry), 0, keepdims=True) - 1.0
        carry = carry + jnp.sum(one, 1, keepdims=True)
    slots = lax.broadcasted_iota(jnp.int32, (capacity, obs), 0).astype(jnp.float32)

    def one_patch(patch, _):
        rank = jnp.where(target_ref[...] == patch, rank_ref[...], -1.0)
        pick = jnp.where(slots == rank, 1.0, 0.0).astype(jnp.bfloat16)
        out_ref[patch] = lax.dot_general(
            data_ref[...], pick, NT, preferred_element_type=jnp.float32
        ).astype(jnp.bfloat16)
        return 0

    lax.fori_loop(0, patches, one_patch, 0)


def dispatch(data, target, patches, capacity):
    rows, obs = data.shape
    return pl.pallas_call(
        functools.partial(dispatch_kernel, patches, capacity),
        out_shape=jax.ShapeDtypeStruct((patches, rows, capacity), jnp.bfloat16),
        in_specs=[pl.BlockSpec(memory_space=pltpu.VMEM)] * 2,
        out_specs=pl.BlockSpec(memory_space=pltpu.VMEM),
        scratch_shapes=[pltpu.VMEM((1, obs), jnp.float32)],
        compiler_params=pltpu.CompilerParams(vmem_limit_bytes=VMEM_LIMIT),
    )(data, target)


def gram_kernel(mem_count, tile_count, got_ref, own_ref, next_ref, prev_ref, own_acc, next_acc, prev_acc):
    tile = pl.program_id(0)
    local = got_ref.shape[2] - INFO
    members = local * mem_count
    values = jnp.concatenate(
        [got_ref[m, 0, :local, :].astype(jnp.float32) for m in range(mem_count)], 0
    )
    obs_mean = jnp.sum(values, 0, keepdims=True) / members
    centred = (values - obs_mean).astype(jnp.bfloat16)
    value = got_ref[0, 0, local : local + 1, :].astype(jnp.float32)
    var = got_ref[0, 0, local + 1 : local + 2, :].astype(jnp.float32)
    shifted = got_ref[0, 0, local + 2 : local + 3, :].astype(jnp.float32)
    is_live = shifted > 0.5
    weight = jnp.where(is_live, 1.0 / jnp.where(is_live, var, 1.0), 0.0)
    position = shifted - 1.0
    innovation = (value - obs_mean).astype(jnp.bfloat16).astype(jnp.float32)
    first = lax.broadcasted_iota(jnp.int32, (16, innovation.shape[1]), 0) == 0
    vector_rows = jnp.where(first, innovation, 0.0).astype(jnp.bfloat16)
    left = jnp.concatenate([centred, vector_rows], 0)
    centred_wide = centred.astype(jnp.float32)
    for offset, acc in ((0.0, own_acc), (-1.0, next_acc), (1.0, prev_acc)):
        distance = (offset * PATCH_CELLS + position + 0.5 - 0.5 * PATCH_CELLS) / PATCH_CELLS
        scale = weight * jnp.exp(-2.0 * distance * distance)
        weighted = (centred_wide * scale).astype(jnp.bfloat16)
        term = lax.dot_general(left, weighted, NT, preferred_element_type=jnp.float32)

        @pl.when(tile == 0)
        def _():
            acc[...] = term

        @pl.when(tile > 0)
        def _():
            acc[...] += term

    @pl.when(tile == tile_count - 1)
    def _():
        own_ref[...] = own_acc[...]
        next_ref[...] = next_acc[...].astype(jnp.bfloat16)
        prev_ref[...] = prev_acc[...].astype(jnp.bfloat16)


def gram_terms(got, mem_count, tile_count):
    rows, capacity = got.shape[2:]
    members = (rows - INFO) * mem_count
    shape = (members + 16, members)
    whole = pl.BlockSpec(shape, lambda t: (0, 0))
    return pl.pallas_call(
        functools.partial(gram_kernel, mem_count, tile_count),
        grid=(tile_count,),
        out_shape=[
            jax.ShapeDtypeStruct(shape, jnp.float32),
            jax.ShapeDtypeStruct(shape, jnp.bfloat16),
            jax.ShapeDtypeStruct(shape, jnp.bfloat16),
        ],
        in_specs=[pl.BlockSpec((mem_count, 1, rows, capacity), lambda t: (0, t, 0, 0))],
        out_specs=[whole] * 3,
        scratch_shapes=[pltpu.VMEM(shape, jnp.float32)] * 3,
        compiler_params=pltpu.CompilerParams(vmem_limit_bytes=VMEM_LIMIT),
    )(got)


def split(a):
    high = a.astype(jnp.bfloat16)
    return high, (a - high.astype(jnp.float32)).astype(jnp.bfloat16)


def product(a, b):
    dot = functools.partial(jnp.dot, preferred_element_type=jnp.float32)
    return dot(a[0], b[0]) + (dot(a[0], b[1]) + dot(a[1], b[0]))


def update_kernel(own_ref, low_ref, high_ref, states_ref, out_ref):
    members = own_ref.shape[1]
    total = own_ref[...] + low_ref[...].astype(jnp.float32) + high_ref[...].astype(jnp.float32)
    diagonal = lax.broadcasted_iota(jnp.int32, (members, members), 0) == lax.broadcasted_iota(
        jnp.int32, (members, members), 1
    )
    identity = jnp.where(diagonal, 1.0, 0.0)
    gram_mat = total[:members] + (members - 1.0) * identity
    gram_vec = total[members:]
    norm_scale = jnp.sqrt(jnp.sum(gram_mat * gram_mat, keepdims=True))
    a = gram_mat / norm_scale
    a_pair = split(a)
    square = product(a_pair, a_pair)
    root = (
        2.25 * identity - 2.4375 * a + 1.6875 * square
        + product(split(square), split(0.0625 * square - 0.5625 * a))
    )
    for _ in range(2):
        root_pair = split(root)
        inner = product(a_pair, split(product(root_pair, root_pair)))
        root = 1.5 * root - 0.5 * product(root_pair, split(inner))
    inv_root = root / jnp.sqrt(norm_scale)
    inv_pair = split(inv_root)
    mean_w = product(split(product(split(gram_vec), inv_pair)), inv_pair)[:1]
    transform = (math.sqrt(members - 1.0) * inv_root + mean_w).astype(jnp.bfloat16)
    states = states_ref[...].astype(jnp.float32)
    state_mean = jnp.sum(states, 0, keepdims=True) / members
    deviation = (states - state_mean).astype(jnp.bfloat16)
    mixed = jnp.dot(transform, deviation, preferred_element_type=jnp.float32)
    out_ref[...] = (state_mean + mixed).astype(jnp.bfloat16)


def update(own, low, high, states):
    return pl.pallas_call(
        update_kernel,
        out_shape=jax.ShapeDtypeStruct(states.shape, jnp.bfloat16),
        in_specs=[pl.BlockSpec(memory_space=pltpu.VMEM)] * 4,
        out_specs=pl.BlockSpec(memory_space=pltpu.VMEM),
        compiler_params=pltpu.CompilerParams(vmem_limit_bytes=VMEM_LIMIT),
    )(own, low, high, states)


def per_device(background, evolved, obs_value, obs_var, obs_patch, obs_pos):
    mem_count = lax.axis_size("mem")
    tile_count = lax.axis_size("tile")
    patches = mem_count * tile_count
    local, obs = evolved.shape
    members = local * mem_count
    cells = background.shape[3]
    capacity = 2 * OBS_PATCH // tile_count
    info = jnp.stack([obs_value, obs_var, (obs_pos + 1).astype(jnp.bfloat16)])
    info = jnp.concatenate([info, jnp.zeros((INFO - 3, obs), jnp.bfloat16)], 0)
    data = jnp.concatenate([evolved, info], 0)
    states = background[:, :, 0, :].transpose(1, 0, 2)
    states = lax.all_to_all(states, "mem", split_axis=0, concat_axis=0, tiled=True)
    send = dispatch(data, obs_patch.reshape(1, obs), patches, capacity)
    got = lax.all_to_all(send, ("mem", "tile"), split_axis=0, concat_axis=0, tiled=True)
    got = got.reshape(mem_count, tile_count, local + INFO, capacity)
    own, to_next, to_prev = gram_terms(got, mem_count, tile_count)
    forward = [(i, (i + 1) % patches) for i in range(patches)]
    backward = [(target, source) for source, target in forward]
    low = lax.ppermute(to_next, ("mem", "tile"), forward)
    high = lax.ppermute(to_prev, ("mem", "tile"), backward)
    updated = update(own, low, high, states.reshape(members, cells))
    back = lax.all_to_all(
        updated.reshape(mem_count, local, cells), "mem", split_axis=0, concat_axis=0, tiled=True
    )
    return back.transpose(1, 0, 2).reshape(background.shape)


def solution(mesh):
    return jax.shard_map(
        per_device,
        mesh=mesh,
        in_specs=(
            P("mem", None, "tile", None),
            P("mem", "tile"),
            P("tile"),
            P("tile"),
            P("tile", None),
            P("tile"),
        ),
        out_specs=P("mem", None, "tile", None),
        check_vma=False,
    )
```

```python
import functools
import math

import jax
import jax.numpy as jnp
from jax import lax
from jax.experimental import pallas as pl
from jax.experimental.pallas import tpu as pltpu
from jax.sharding import PartitionSpec as P

PATCH_CELLS = 128
OBS_PATCH = 1024
INFO = 16
VMEM_LIMIT = 48 * 1024 * 1024
MESH = pl.DeviceIdType.MESH
NT = (((1,), (1,)), ((), ()))


def rank_of(patches, target_ref, rank_ref):
    obs = target_ref.shape[1]
    chunk = 256
    upper = (
        lax.broadcasted_iota(jnp.int32, (chunk, chunk), 0)
        <= lax.broadcasted_iota(jnp.int32, (chunk, chunk), 1)
    ).astype(jnp.float32).astype(jnp.bfloat16)
    names = lax.broadcasted_iota(jnp.int32, (patches, chunk), 0)
    carry = jnp.zeros((patches, 1), jnp.float32)
    for start in range(0, obs, chunk):
        hit = names == target_ref[:, start : start + chunk]
        one = jnp.where(hit, 1.0, 0.0)
        run = jnp.dot(one.astype(jnp.bfloat16), upper, preferred_element_type=jnp.float32)
        rank_ref[:, start : start + chunk] = jnp.sum(one * (run + carry), 0, keepdims=True) - 1.0
        carry = carry + jnp.sum(one, 1, keepdims=True)


def add_gram(mem_count, tile_count, tile, got_ref, accs):
    local = got_ref.shape[1] - INFO
    members = local * mem_count
    values = jnp.concatenate(
        [got_ref[m * tile_count + tile][:local].astype(jnp.float32) for m in range(mem_count)], 0
    )
    info = got_ref[tile][local:].astype(jnp.float32)
    obs_mean = jnp.sum(values, 0, keepdims=True) / members
    centred = (values - obs_mean).astype(jnp.bfloat16)
    shifted = info[2:3]
    is_live = shifted > 0.5
    weight = jnp.where(is_live, 1.0 / jnp.where(is_live, info[1:2], 1.0), 0.0)
    position = shifted - 1.0
    innovation = info[0:1] - obs_mean
    first = lax.broadcasted_iota(jnp.int32, (INFO, innovation.shape[1]), 0) == 0
    vector_rows = jnp.where(first, innovation, 0.0).astype(jnp.bfloat16)
    left = jnp.concatenate([centred, vector_rows], 0)
    centred_wide = centred.astype(jnp.float32)
    for offset, acc in zip((0.0, -1.0, 1.0), accs):
        distance = (offset * PATCH_CELLS + position + 0.5 - 0.5 * PATCH_CELLS) / PATCH_CELLS
        scale = weight * jnp.exp(-2.0 * distance * distance)
        weighted = (centred_wide * scale).astype(jnp.bfloat16)
        acc[...] += lax.dot_general(left, weighted, NT, preferred_element_type=jnp.float32)


def split(a):
    high = a.astype(jnp.bfloat16)
    return high, (a - high.astype(jnp.float32)).astype(jnp.bfloat16)


def product(a, b):
    dot = functools.partial(jnp.dot, preferred_element_type=jnp.float32)
    return dot(a[0], b[0]) + (dot(a[0], b[1]) + dot(a[1], b[0]))


def transform_of(total):
    members = total.shape[1]
    diagonal = lax.broadcasted_iota(jnp.int32, (members, members), 0) == lax.broadcasted_iota(
        jnp.int32, (members, members), 1
    )
    identity = jnp.where(diagonal, 1.0, 0.0)
    gram_mat = total[:members] + (members - 1.0) * identity
    gram_vec = total[members:]
    norm_scale = jnp.sqrt(jnp.sum(gram_mat * gram_mat, keepdims=True))
    a = gram_mat / norm_scale
    a_pair = split(a)
    square = product(a_pair, a_pair)
    root = (
        2.25 * identity - 2.4375 * a + 1.6875 * square
        + product(split(square), split(0.0625 * square - 0.5625 * a))
    )
    for _ in range(2):
        root_pair = split(root)
        inner = product(a_pair, split(product(root_pair, root_pair)))
        root = 1.5 * root - 0.5 * product(root_pair, split(inner))
    inv_root = root / jnp.sqrt(norm_scale)
    inv_pair = split(inv_root)
    mean_w = product(split(product(split(gram_vec), inv_pair)), inv_pair)[:1]
    return (math.sqrt(members - 1.0) * inv_root + mean_w).astype(jnp.bfloat16)


def analysis_kernel(
    mem_count, tile_count,
    back_ref, evolved_ref, info_ref, target_ref, out_ref,
    data, rank_ref, send, got, own_acc, next_acc, prev_acc, next_send, prev_send, low, high, states, updated,
    send_sem, recv_sem, side_send, side_recv, state_send, state_recv, out_send, out_recv, own_sem,
):
    patches = mem_count * tile_count
    local, obs = evolved_ref.shape
    members = local * mem_count
    capacity = send.shape[2]
    mem, tile = lax.axis_index("mem"), lax.axis_index("tile")
    me = mem * tile_count + tile

    def device(index):
        return (lax.div(index, tile_count), lax.rem(index, tile_count))

    barrier = pltpu.get_barrier_semaphore()

    def greet(step, _):
        pl.semaphore_signal(
            barrier, inc=1, device_id=device(lax.rem(me + step, patches)), device_id_type=MESH
        )
        return 0

    lax.fori_loop(1, patches, greet, 0)
    data[:local] = evolved_ref[...]
    data[local:] = info_ref[...]
    rank_of(patches, target_ref, rank_ref)
    pl.semaphore_wait(barrier, patches - 1)

    def tile_step(index):
        return tile_count // 2 + lax.div(index + 1, 2) * (1 - 2 * lax.rem(index, 2))

    def block_copy(partner, slot):
        return pltpu.make_async_remote_copy(
            src_ref=send.at[partner], dst_ref=got.at[slot],
            send_sem=send_sem.at[partner], recv_sem=recv_sem.at[slot],
            device_id=device(partner), device_id_type=MESH,
        )

    def partner_of(step):
        to_tile = lax.rem(tile + tile_step(lax.div(step, mem_count)), tile_count)
        to_mem = lax.rem(mem + mem_count - 1 - lax.rem(step, mem_count), mem_count)
        return to_mem * tile_count + to_tile

    slots = lax.broadcasted_iota(jnp.int32, (capacity, obs), 0).astype(jnp.float32)

    def place(patch):
        rank = jnp.where(target_ref[...] == patch, rank_ref[...], -1.0)
        pick = jnp.where(slots == rank, 1.0, 0.0).astype(jnp.bfloat16)
        return lax.dot_general(data[...], pick, NT, preferred_element_type=jnp.float32).astype(jnp.bfloat16)

    def send_one(step, _):
        partner = partner_of(step)
        send[partner] = place(partner)
        block_copy(partner, me).start()
        return 0

    lax.fori_loop(0, patches - 1, send_one, 0)
    got[me] = place(me)

    def state_copy(distance):
        partner = lax.rem(mem + distance, mem_count)
        return pltpu.make_async_remote_copy(
            src_ref=back_ref.at[partner], dst_ref=states.at[mem],
            send_sem=state_send.at[distance], recv_sem=state_recv.at[distance],
            device_id=(partner, tile), device_id_type=MESH,
        )

    for distance in range(1, mem_count):
        state_copy(distance).start()
    states[mem] = back_ref[mem]

    for acc in (own_acc, next_acc, prev_acc):
        acc[...] = jnp.zeros_like(acc)
    accs = (own_acc, next_acc, prev_acc)

    def take_tile(index, _):
        source_tile = lax.rem(tile + tile_count - tile_step(index), tile_count)
        for m in range(mem_count):
            source = m * tile_count + source_tile
            block_copy(source, source).wait_recv()
        add_gram(mem_count, tile_count, source_tile, got, accs)
        return 0

    lax.fori_loop(0, tile_count - 1, take_tile, 0)
    for distance in range(1, mem_count):
        source = lax.rem(mem + distance, mem_count) * tile_count + tile
        block_copy(source, source).wait_recv()
    add_gram(mem_count, tile_count, tile, got, accs)

    next_send[...] = next_acc[...].astype(jnp.bfloat16)
    prev_send[...] = prev_acc[...].astype(jnp.bfloat16)

    def side_copy(block, target, which, distance):
        return pltpu.make_async_remote_copy(
            src_ref=block, dst_ref=target,
            send_sem=side_send.at[which], recv_sem=side_recv.at[which],
            device_id=device(lax.rem(me + distance, patches)), device_id_type=MESH,
        )

    sides = (side_copy(next_send, low, 0, 1), side_copy(prev_send, high, 1, patches - 1))
    for side in sides:
        side.start()

    for distance in range(1, mem_count):
        state_copy(distance).wait()
    wide = states[...].reshape(members, states.shape[2]).astype(jnp.float32)
    state_mean = jnp.sum(wide, 0, keepdims=True) / members
    deviation = (wide - state_mean).astype(jnp.bfloat16)
    for side in sides:
        side.wait()
    total = own_acc[...] + low[...].astype(jnp.float32) + high[...].astype(jnp.float32)
    transform = transform_of(total)
    mixed = jnp.dot(transform, deviation, preferred_element_type=jnp.float32)
    updated[...] = (state_mean + mixed).astype(jnp.bfloat16).reshape(updated.shape)

    def out_copy(distance):
        partner = lax.rem(mem + distance, mem_count)
        return pltpu.make_async_remote_copy(
            src_ref=updated.at[partner], dst_ref=out_ref.at[mem],
            send_sem=out_send.at[distance], recv_sem=out_recv.at[distance],
            device_id=(partner, tile), device_id_type=MESH,
        )

    for distance in range(1, mem_count):
        out_copy(distance).start()
    mine = pltpu.make_async_copy(updated.at[mem], out_ref.at[mem], own_sem)
    mine.start()
    mine.wait()
    for distance in range(1, mem_count):
        out_copy(distance).wait()

    def finish(step, _):
        block_copy(partner_of(step), me).wait_send()
        return 0

    lax.fori_loop(0, patches - 1, finish, 0)


def per_device(background, evolved, obs_value, obs_var, obs_patch, obs_pos):
    mem_count = lax.axis_size("mem")
    tile_count = lax.axis_size("tile")
    patches = mem_count * tile_count
    local, obs = evolved.shape
    members = local * mem_count
    cells = background.shape[3]
    capacity = 2 * OBS_PATCH // tile_count
    info = jnp.stack([obs_value, obs_var, (obs_pos + 1).astype(jnp.bfloat16)])
    info = jnp.concatenate([info, jnp.zeros((INFO - 3, obs), jnp.bfloat16)], 0)
    states = background[:, :, 0, :].transpose(1, 0, 2)
    rows = local + INFO
    gram_shape = (members + INFO, members)
    dma = pltpu.SemaphoreType.DMA
    analysis = pl.pallas_call(
        functools.partial(analysis_kernel, mem_count, tile_count),
        out_shape=jax.ShapeDtypeStruct((mem_count, local, cells), jnp.bfloat16),
        in_specs=[pl.BlockSpec(memory_space=pltpu.VMEM)] * 4,
        out_specs=pl.BlockSpec(memory_space=pl.ANY),
        scratch_shapes=[
            pltpu.VMEM((rows, obs), jnp.bfloat16),
            pltpu.VMEM((1, obs), jnp.float32),
            pltpu.VMEM((patches, rows, capacity), jnp.bfloat16),
            pltpu.VMEM((patches, rows, capacity), jnp.bfloat16),
            *[pltpu.VMEM(gram_shape, jnp.float32)] * 3,
            *[pltpu.VMEM(gram_shape, jnp.bfloat16)] * 4,
            *[pltpu.VMEM((mem_count, local, cells), jnp.bfloat16)] * 2,
            dma((patches,)),
            dma((patches,)),
            dma((2,)),
            dma((2,)),
            *[dma((mem_count,))] * 4,
            dma(()),
        ],
        compiler_params=pltpu.CompilerParams(
            collective_id=0, has_side_effects=True, vmem_limit_bytes=VMEM_LIMIT
        ),
    )(states, evolved, info, obs_patch.reshape(1, obs))
    return analysis.transpose(1, 0, 2).reshape(background.shape)


def solution(mesh):
    return jax.shard_map(
        per_device,
        mesh=mesh,
        in_specs=(
            P("mem", None, "tile", None),
            P("mem", "tile"),
            P("tile"),
            P("tile"),
            P("tile", None),
            P("tile"),
        ),
        out_specs=P("mem", None, "tile", None),
        check_vma=False,
    )
```

```python
import functools
import math

import jax
import jax.numpy as jnp
from jax import lax
from jax.experimental import pallas as pl
from jax.experimental.pallas import tpu as pltpu
from jax.sharding import PartitionSpec as P

PATCH_CELLS = 128
OBS_PATCH = 1024
INFO = 16
VMEM_LIMIT = 48 * 1024 * 1024
MESH = pl.DeviceIdType.MESH
NT = (((1,), (1,)), ((), ()))


def rank_of(patches, target_ref, rank_ref):
    obs = target_ref.shape[1]
    chunk = 256
    upper = (
        lax.broadcasted_iota(jnp.int32, (chunk, chunk), 0)
        <= lax.broadcasted_iota(jnp.int32, (chunk, chunk), 1)
    ).astype(jnp.float32).astype(jnp.bfloat16)
    names = lax.broadcasted_iota(jnp.int32, (patches, chunk), 0)
    carry = jnp.zeros((patches, 1), jnp.float32)
    for start in range(0, obs, chunk):
        hit = names == target_ref[:, start : start + chunk]
        one = jnp.where(hit, 1.0, 0.0)
        run = jnp.dot(one.astype(jnp.bfloat16), upper, preferred_element_type=jnp.float32)
        rank_ref[:, start : start + chunk] = jnp.sum(one * (run + carry), 0, keepdims=True) - 1.0
        carry = carry + jnp.sum(one, 1, keepdims=True)


def add_gram(mem_count, tile_count, tile, got_ref, accs):
    local = got_ref.shape[1] - INFO
    members = local * mem_count
    values = jnp.concatenate(
        [got_ref[m * tile_count + tile][:local].astype(jnp.float32) for m in range(mem_count)], 0
    )
    info = got_ref[tile][local:].astype(jnp.float32)
    obs_mean = jnp.sum(values, 0, keepdims=True) / members
    centred = (values - obs_mean).astype(jnp.bfloat16)
    shifted = info[2:3]
    is_live = shifted > 0.5
    weight = jnp.where(is_live, 1.0 / jnp.where(is_live, info[1:2], 1.0), 0.0)
    position = shifted - 1.0
    innovation = info[0:1] - obs_mean
    first = lax.broadcasted_iota(jnp.int32, (INFO, innovation.shape[1]), 0) == 0
    vector_rows = jnp.where(first, innovation, 0.0).astype(jnp.bfloat16)
    left = jnp.concatenate([centred, vector_rows], 0)
    centred_wide = centred.astype(jnp.float32)
    for offset, acc in zip((0.0, -1.0, 1.0), accs):
        distance = (offset * PATCH_CELLS + position + 0.5 - 0.5 * PATCH_CELLS) / PATCH_CELLS
        scale = weight * jnp.exp(-2.0 * distance * distance)
        weighted = (centred_wide * scale).astype(jnp.bfloat16)
        acc[...] += lax.dot_general(left, weighted, NT, preferred_element_type=jnp.float32)


def split(a):
    high = a.astype(jnp.bfloat16)
    return high, (a - high.astype(jnp.float32)).astype(jnp.bfloat16)


def product(a, b):
    dot = functools.partial(jnp.dot, preferred_element_type=jnp.float32)
    return dot(a[0], b[0]) + (dot(a[0], b[1]) + dot(a[1], b[0]))


def transform_of(total):
    members = total.shape[1]
    diagonal = lax.broadcasted_iota(jnp.int32, (members, members), 0) == lax.broadcasted_iota(
        jnp.int32, (members, members), 1
    )
    identity = jnp.where(diagonal, 1.0, 0.0)
    gram_mat = total[:members] + (members - 1.0) * identity
    gram_vec = total[members:]
    norm_scale = jnp.sqrt(jnp.sum(gram_mat * gram_mat, keepdims=True))
    a = gram_mat / norm_scale
    a_pair = split(a)
    square = product(a_pair, a_pair)
    root = (
        2.25 * identity - 2.4375 * a + 1.6875 * square
        + product(split(square), split(0.0625 * square - 0.5625 * a))
    )
    for _ in range(2):
        root_pair = split(root)
        inner = product(a_pair, split(product(root_pair, root_pair)))
        root = 1.5 * root - 0.5 * product(root_pair, split(inner))
    inv_root = root / jnp.sqrt(norm_scale)
    inv_pair = split(inv_root)
    mean_w = product(split(product(split(gram_vec), inv_pair)), inv_pair)[:1]
    return (math.sqrt(members - 1.0) * inv_root + mean_w).astype(jnp.bfloat16)


def analysis_kernel(
    mem_count, tile_count,
    back_ref, evolved_ref, info_ref, target_ref, out_ref,
    data, rank_ref, send, got, own_acc, next_acc, prev_acc, next_send, prev_send, low, high, states, updated,
    send_sem, recv_sem, side_send, side_recv, state_send, state_recv, out_send, out_recv, own_sem,
):
    patches = mem_count * tile_count
    local, obs = evolved_ref.shape
    members = local * mem_count
    capacity = send.shape[2]
    mem, tile = lax.axis_index("mem"), lax.axis_index("tile")
    me = mem * tile_count + tile

    def device(index):
        return (lax.div(index, tile_count), lax.rem(index, tile_count))

    barrier = pltpu.get_barrier_semaphore()

    def greet(step, _):
        pl.semaphore_signal(
            barrier, inc=1, device_id=device(lax.rem(me + step, patches)), device_id_type=MESH
        )
        return 0

    lax.fori_loop(1, patches, greet, 0)
    data[:local] = evolved_ref[...]
    data[local:] = info_ref[...]
    rank_of(patches, target_ref, rank_ref)
    pl.semaphore_wait(barrier, patches - 1)

    def tile_step(index):
        return tile_count // 2 + lax.div(index + 1, 2) * (1 - 2 * lax.rem(index, 2))

    def block_copy(partner, slot):
        return pltpu.make_async_remote_copy(
            src_ref=send.at[partner], dst_ref=got.at[slot],
            send_sem=send_sem.at[partner], recv_sem=recv_sem.at[slot],
            device_id=device(partner), device_id_type=MESH,
        )

    def partner_of(step):
        to_tile = lax.rem(tile + tile_step(lax.div(step, mem_count)), tile_count)
        to_mem = lax.rem(mem + mem_count - 1 - lax.rem(step, mem_count), mem_count)
        return to_mem * tile_count + to_tile

    slots = lax.broadcasted_iota(jnp.int32, (capacity, obs), 0).astype(jnp.float32)

    def place(patch):
        rank = jnp.where(target_ref[...] == patch, rank_ref[...], -1.0)
        pick = jnp.where(slots == rank, 1.0, 0.0).astype(jnp.bfloat16)
        return lax.dot_general(data[...], pick, NT, preferred_element_type=jnp.float32).astype(jnp.bfloat16)

    def send_one(step, _):
        partner = partner_of(step)
        send[partner] = place(partner)
        block_copy(partner, me).start()
        return 0

    lax.fori_loop(0, patches - 1, send_one, 0)
    got[me] = place(me)

    def state_copy(distance):
        partner = lax.rem(mem + distance, mem_count)
        return pltpu.make_async_remote_copy(
            src_ref=back_ref.at[partner], dst_ref=states.at[mem],
            send_sem=state_send.at[distance], recv_sem=state_recv.at[distance],
            device_id=(partner, tile), device_id_type=MESH,
        )

    for distance in range(1, mem_count):
        state_copy(distance).start()
    states[mem] = back_ref[mem]

    for acc in (own_acc, next_acc, prev_acc):
        acc[...] = jnp.zeros_like(acc)
    accs = (own_acc, next_acc, prev_acc)

    def take_tile(index, _):
        source_tile = lax.rem(tile + tile_count - tile_step(index), tile_count)
        for m in range(mem_count):
            source = m * tile_count + source_tile
            block_copy(source, source).wait_recv()
        add_gram(mem_count, tile_count, source_tile, got, accs)
        return 0

    lax.fori_loop(0, tile_count - 1, take_tile, 0)
    for distance in range(1, mem_count):
        source = lax.rem(mem + distance, mem_count) * tile_count + tile
        block_copy(source, source).wait_recv()
    add_gram(mem_count, tile_count, tile, got, accs)

    next_send[...] = next_acc[...].astype(jnp.bfloat16)
    prev_send[...] = prev_acc[...].astype(jnp.bfloat16)

    def side_copy(block, target, which, distance):
        return pltpu.make_async_remote_copy(
            src_ref=block, dst_ref=target,
            send_sem=side_send.at[which], recv_sem=side_recv.at[which],
            device_id=device(lax.rem(me + distance, patches)), device_id_type=MESH,
        )

    half = members // 2
    parts = ((pl.ds(half, half + INFO), pl.ds(0, members)), (pl.ds(0, half), pl.ds(0, half)))
    sides = [
        side_copy(block.at[part], target.at[part], 2 * k + side, distance)
        for k, part in enumerate(parts)
        for side, (block, target, distance) in enumerate(
            ((next_send, low, 1), (prev_send, high, patches - 1))
        )
    ]
    for side in sides:
        side.start()

    for distance in range(1, mem_count):
        state_copy(distance).wait()
    wide = states[...].reshape(members, states.shape[2]).astype(jnp.float32)
    state_mean = jnp.sum(wide, 0, keepdims=True) / members
    deviation = (wide - state_mean).astype(jnp.bfloat16)
    for side in sides:
        side.wait()
    below, top = [low[part].astype(jnp.float32) + high[part].astype(jnp.float32) for part in parts]
    side_sum = jnp.concatenate([jnp.concatenate([top, below[:half, :half].T], 1), below], 0)
    total = own_acc[...] + side_sum
    transform = transform_of(total)
    mixed = jnp.dot(transform, deviation, preferred_element_type=jnp.float32)
    updated[...] = (state_mean + mixed).astype(jnp.bfloat16).reshape(updated.shape)

    def out_copy(distance):
        partner = lax.rem(mem + distance, mem_count)
        return pltpu.make_async_remote_copy(
            src_ref=updated.at[partner], dst_ref=out_ref.at[mem],
            send_sem=out_send.at[distance], recv_sem=out_recv.at[distance],
            device_id=(partner, tile), device_id_type=MESH,
        )

    for distance in range(1, mem_count):
        out_copy(distance).start()
    mine = pltpu.make_async_copy(updated.at[mem], out_ref.at[mem], own_sem)
    mine.start()
    mine.wait()
    for distance in range(1, mem_count):
        out_copy(distance).wait()

    def finish(step, _):
        block_copy(partner_of(step), me).wait_send()
        return 0

    lax.fori_loop(0, patches - 1, finish, 0)


def per_device(background, evolved, obs_value, obs_var, obs_patch, obs_pos):
    mem_count = lax.axis_size("mem")
    tile_count = lax.axis_size("tile")
    patches = mem_count * tile_count
    local, obs = evolved.shape
    members = local * mem_count
    cells = background.shape[3]
    capacity = 2 * OBS_PATCH // tile_count
    info = jnp.stack([obs_value, obs_var, (obs_pos + 1).astype(jnp.bfloat16)])
    info = jnp.concatenate([info, jnp.zeros((INFO - 3, obs), jnp.bfloat16)], 0)
    states = background[:, :, 0, :].transpose(1, 0, 2)
    rows = local + INFO
    gram_shape = (members + INFO, members)
    dma = pltpu.SemaphoreType.DMA
    analysis = pl.pallas_call(
        functools.partial(analysis_kernel, mem_count, tile_count),
        out_shape=jax.ShapeDtypeStruct((mem_count, local, cells), jnp.bfloat16),
        in_specs=[pl.BlockSpec(memory_space=pltpu.VMEM)] * 4,
        out_specs=pl.BlockSpec(memory_space=pl.ANY),
        scratch_shapes=[
            pltpu.VMEM((rows, obs), jnp.bfloat16),
            pltpu.VMEM((1, obs), jnp.float32),
            pltpu.VMEM((patches, rows, capacity), jnp.bfloat16),
            pltpu.VMEM((patches, rows, capacity), jnp.bfloat16),
            *[pltpu.VMEM(gram_shape, jnp.float32)] * 3,
            *[pltpu.VMEM(gram_shape, jnp.bfloat16)] * 4,
            *[pltpu.VMEM((mem_count, local, cells), jnp.bfloat16)] * 2,
            dma((patches,)),
            dma((patches,)),
            dma((4,)),
            dma((4,)),
            *[dma((mem_count,))] * 4,
            dma(()),
        ],
        compiler_params=pltpu.CompilerParams(
            collective_id=0, has_side_effects=True, vmem_limit_bytes=VMEM_LIMIT
        ),
    )(states, evolved, info, obs_patch.reshape(1, obs))
    return analysis.transpose(1, 0, 2).reshape(background.shape)


def solution(mesh):
    return jax.shard_map(
        per_device,
        mesh=mesh,
        in_specs=(
            P("mem", None, "tile", None),
            P("mem", "tile"),
            P("tile"),
            P("tile"),
            P("tile", None),
            P("tile"),
        ),
        out_specs=P("mem", None, "tile", None),
        check_vma=False,
    )
```
